1024 devices in a mesh: dp: 64 (over z, core), expert: 16 (over x, y).
Axes of the slice: x: 4, y: 4, z: 32, core: 2. Of those that a mesh axis runs over, the one named last changes fastest.
Arguments:
- tokens: bfloat16 [768, 3072], P('expert', 'dp'), may hold values from -6 to 6
- cotangent: bfloat16 [768, 3072], P('expert', 'dp'), may hold values from -6 to 6
- routes: int32 [768, 4], P('expert'), may hold values from 0 to 15, all different within a row; in each aligned block of 48 rows (0 to 47, 48 to 95, ...) at most 16 rows name the same one
- route_weights: float32 [768, 4], P('expert'), may hold values from 0.05 to 0.6
- gate_up: bfloat16 [16, 2, 5376, 3072], P('expert', None, 'dp'), may hold values from -0.109375 to 0.109375
- down_proj: bfloat16 [16, 5376, 3072], P('expert', 'dp'), may hold values from -0.078125 to 0.078125
Outputs:
- grad_tokens: bfloat16 [768, 3072], P('expert', 'dp')
- grad_gate_up: bfloat16 [16, 2, 5376, 3072], P('expert', None, 'dp')
- grad_down: bfloat16 [16, 5376, 3072], P('expert', 'dp')
The draws below stay inside these ranges and needn't reach their ends.
Inputs may be any that keep to these rules, and one draw needn't show every extreme that they name: `routes`: each token names 4 different experts. Within the tokens of one index of the expert axis (aligned blocks of 48 rows) no expert is named more than 16 times, and in every draw some expert is named exactly 16 times in some block.
All inputs are finite; a program needn't handle non-finite values.
Results may differ from the reference program's by a relative error of at most 0.0064.
Values may be sent and summed in bfloat16 or wider, within the bound.
No kernel may reach another device: no remote copies, remote signals or barrier semaphores. Data moves between devices by JAX's collectives and lax.ppermute only.
A program may use at most 32 MiB of HBM per device.

```python
import math
import jax
import jax.numpy as jnp
import numpy as np
from jax import lax

D = 3072
HID = 5376
TOP = 4
TOK_DEV = 48
EXPERTS = 16
CAP = 16
TOKENS = 768
N_EXPERT = 16


def block_scale(stream_key, shape, cuts, least, largest):
    gain = 1.0
    for position, blocks in cuts:
        draws = jax.random.uniform(jax.random.fold_in(jax.random.fold_in(stream_key, 6), position), (blocks,), jnp.float32, least / len(cuts), largest / len(cuts))
        gain = gain * jnp.repeat(jnp.exp(draws), shape[position] // blocks).reshape((-1,) + (1,) * (len(shape) - 1 - position))
    return gain


def shared_out(stream_key, own, number, rows, amount, top, most, lean):
    order = jax.random.permutation(stream_key, amount)
    heavy_load, common = load_shares(amount, rows * top, most, lean, True), load_shares(amount, rows * top, most, lean, False)
    places = jnp.arange(amount)

    def named(lengths, rotation):
        used = int((lengths > 0).sum())
        fixed = max(1, used // 4)
        moved = fixed + (places - fixed + rotation * (used - fixed)) % max(1, amount - fixed)
        return jnp.zeros((amount,), jnp.int32).at[order[jnp.where(places < fixed, places, moved)]].set(jnp.asarray(lengths, jnp.int32))

    lengths = jnp.where(number % 4 == 0, named(heavy_load, number // 4), named(common, number - number // 4 - 1))
    mixed = jax.random.permutation(jax.random.fold_in(own, 3), amount)
    source_of, receiver = mixed[0:amount // 2 * 2:2], mixed[1:amount // 2 * 2:2]
    room = jnp.minimum(lengths[source_of] - 1, most - lengths[receiver]) // 2
    room = jnp.where((source_of == order[0]) | (receiver == order[0]) | (lengths[receiver] == 0), 0, jnp.maximum(room, 0))
    moved = jax.random.randint(jax.random.fold_in(own, 4), (amount // 2,), 0, 1 << 20) % (room + 1)
    lengths = lengths.at[source_of].add(-moved).at[receiver].add(moved)
    members = jnp.searchsorted(jnp.cumsum(lengths), jnp.arange(rows * top), side="right").astype(jnp.int32)
    grid = members.reshape(top, rows).T
    grid = grid[jax.random.permutation(jax.random.fold_in(own, 1), rows)]
    rotation = jax.random.randint(jax.random.fold_in(own, 2), (rows, 1), 0, top)
    return jnp.take_along_axis(grid, (jnp.arange(top)[None, :] + rotation) % top, axis=1)


def load_shares(amount, total, bound, skew, full):
    loads = [(1 << 20) // math.isqrt(grade ** skew) + 1 for grade in range(1, amount + 1)]
    largest = bound if full else min(bound, max(-(-total // amount), total * loads[0] // sum(loads)))
    least = 1 if total - largest >= amount - 1 else 0
    given, spare = [largest] + [least] * (amount - 1), total - largest - least * (amount - 1)
    while spare > 0:
        free = [i for i in range(1, amount) if given[i] < largest] or [i for i in range(1, amount) if given[i] < bound]
        mass, budget = sum([loads[i] for i in free]), spare
        for i in free:
            more = min(bound - given[i], max(1, budget * loads[i] // mass), spare)
            given[i] = given[i] + more
            spare = spare - more
    return np.array(given)


def noise(key, shape, width, reach, pieces=(), held_as=jnp.bfloat16):
    drawn = jax.random.normal(key, shape, jnp.float32) * width
    if len(pieces) > 0:
        drawn = block_scale(key, shape, pieces, -0.22, 0.18) * drawn
    return jnp.clip(drawn, min=-reach, max=reach).astype(held_as)


def setup_inputs(seed: int = 0) -> dict:
    arg_keys = jax.random.split(jax.random.key(seed), 7)
    tokens = noise(arg_keys[0], (TOKENS, D), 1.0, 6.0, ((0, 16), (1, 64)))
    cotangent = noise(arg_keys[1], (TOKENS, D), 1.0, 6.0, ((0, 16), (1, 64)))
    routes_keys = jax.random.split(jax.random.fold_in(arg_keys[2], 1), TOKENS // TOK_DEV)
    routes_turns = jax.random.permutation(jax.random.fold_in(arg_keys[2], 3), TOKENS // TOK_DEV)
    routes = jax.vmap(lambda own, number: shared_out(jax.random.fold_in(arg_keys[2], 2), own, number, TOK_DEV, EXPERTS, TOP, CAP, 1))(routes_keys, routes_turns).reshape((TOKENS, TOP))
    route_weights = jnp.clip(jnp.exp(math.log(0.6) - 2.4849067 * jax.random.uniform(arg_keys[3], (TOKENS, TOP), jnp.float32) ** block_scale(arg_keys[3], (TOKENS, TOP), ((0, 16),), -0.2, 0.2)), 0.05, 0.6)
    gate_up = noise(arg_keys[4], (EXPERTS, 2, HID, D), D ** -0.5, 0.109375, ((0, 16), (2, 64)))
    down_proj = noise(arg_keys[5], (EXPERTS, HID, D), HID ** -0.5, 0.078125, ((0, 16), (1, 64)))
    return dict(tokens=tokens, cotangent=cotangent, routes=routes, route_weights=route_weights, gate_up=gate_up, down_proj=down_proj)


def reference(tokens, cotangent, routes, route_weights, gate_up, down_proj):
    flat_routes = routes.reshape(-1)
    assigned = flat_routes.shape[0]
    limit = min(CAP * N_EXPERT, assigned)
    flat_weights = route_weights.reshape(-1)
    order_base = jnp.arange(assigned, dtype=jnp.int32)

    def one_expert(total, inputs):
        expert_id, weights_in, weights_out = inputs
        chosen = flat_routes == expert_id
        sort_keys = jnp.where(chosen, 0, assigned).astype(jnp.int32) + order_base
        picked = jnp.argsort(sort_keys)[:limit].astype(jnp.int32)
        count = jnp.sum(chosen.astype(jnp.int32))
        valid = jnp.arange(limit, dtype=jnp.int32) < count
        token_ids = (picked // TOP).astype(jnp.int32)
        rows = jnp.where(valid[:, None], tokens[token_ids], jnp.zeros((), tokens.dtype))
        grad_rows = jnp.where(valid[:, None], cotangent[token_ids], jnp.zeros((), cotangent.dtype))
        scales = jnp.where(valid, flat_weights[picked], jnp.zeros((), jnp.float32))
        scaled_grad = (scales[:, None] * grad_rows.astype(jnp.float32)).astype(jnp.bfloat16)
        gate_part = jnp.dot(rows, weights_in[0].T, preferred_element_type=jnp.float32)
        up_part = jnp.dot(rows, weights_in[1].T, preferred_element_type=jnp.float32)
        sig_gate = jax.nn.sigmoid(gate_part)
        activated = (gate_part * sig_gate * up_part).astype(jnp.bfloat16)
        back_grad = jnp.dot(scaled_grad, weights_out.T, preferred_element_type=jnp.float32)
        grad_gate = (back_grad * up_part * sig_gate * (1.0 + gate_part * (1.0 - sig_gate))).astype(jnp.bfloat16)
        grad_up = (back_grad * gate_part * sig_gate).astype(jnp.bfloat16)
        token_part = (jnp.dot(grad_gate, weights_in[0], preferred_element_type=jnp.float32)
                      + jnp.dot(grad_up, weights_in[1], preferred_element_type=jnp.float32)).astype(jnp.bfloat16)
        grad_in = jnp.stack([jnp.dot(grad_gate.T, rows, preferred_element_type=jnp.float32),
                             jnp.dot(grad_up.T, rows, preferred_element_type=jnp.float32)]).astype(jnp.bfloat16)
        grad_out = jnp.dot(activated.T, scaled_grad, preferred_element_type=jnp.float32).astype(jnp.bfloat16)
        total = total.at[token_ids].add(jnp.where(valid[:, None], token_part.astype(jnp.float32), jnp.zeros((), jnp.float32)))
        return total, (grad_in, grad_out)

    start = jnp.zeros(tokens.shape, jnp.float32)
    total, (grad_gate_up, grad_down) = lax.scan(
        one_expert, start, (jnp.arange(EXPERTS, dtype=jnp.int32), gate_up, down_proj))
    return total.astype(jnp.bfloat16), grad_gate_up, grad_down
```

```python
import jax
import jax.numpy as jnp
import numpy as np
from jax import lax
from jax.sharding import Mesh, PartitionSpec as P

FAR, NEAR, CORE, EXPERT = "zfar", "znear", "core", "expert"
Z = (FAR, NEAR)
F32, BF16 = jnp.float32, jnp.bfloat16


def dot(left, right, contract):
    return lax.dot_general(left, right, (contract, ((), ())), preferred_element_type=F32)


def exchange(value, axes):
    return lax.all_to_all(value, axes, split_axis=0, concat_axis=0, tiled=True)


def swap_cores(value):
    return lax.ppermute(value, CORE, [(0, 1), (1, 0)])


def slot_tables(routes, route_weights, experts, capacity):
    tok_count, top_count = routes.shape
    slot_total = experts * capacity
    flat_routes = routes.reshape(-1)
    hot_expert = (flat_routes[:, None] == jnp.arange(experts, dtype=jnp.int32)[None, :]).astype(
        jnp.int32
    )
    earlier = jnp.cumsum(hot_expert, axis=0) - hot_expert
    position = jnp.sum(earlier * hot_expert, axis=1)
    slot_ids = flat_routes * capacity + position
    slot_table = (slot_ids[None, :] == jnp.arange(slot_total, dtype=jnp.int32)[:, None]).astype(F32)
    slot_token = slot_table.reshape(slot_total, tok_count, top_count).sum(axis=2)
    slot_scale = jnp.sum(slot_table * route_weights.reshape(-1)[None, :], axis=1)
    return slot_token.astype(BF16), slot_scale


def on_device(tokens, cotangent, routes, route_weights, gate_up, down_proj):
    far, near, experts = (lax.axis_size(name) for name in (FAR, NEAR, EXPERT))
    core = lax.axis_index(CORE)
    tok_count, top_count = routes.shape
    feat = tokens.shape[1]
    width = feat * far * near * 2
    capacity = min(tok_count, tok_count * top_count * 4 // (3 * experts))
    slots = experts * capacity
    picker, slot_scale = slot_tables(routes, route_weights, experts, capacity)

    both = jnp.stack([tokens.T, cotangent.T])
    sent = jnp.broadcast_to(both[None], (far, 2, feat, tok_count)).reshape(far * 2, feat, tok_count)
    column = exchange(sent, (FAR, CORE))
    column = jnp.broadcast_to(column[None], (near,) + column.shape)
    column = exchange(column, NEAR)
    column = column.reshape(near, far, 2, feat, tok_count).transpose(1, 0, 2, 3, 4)
    column = column.reshape(width, tok_count)

    rows = dot(picker, column, ((1,), (1,))).astype(BF16)
    scale = jnp.where(core == 0, 1.0, slot_scale)
    rows = (scale[:, None] * rows.astype(F32)).astype(BF16)
    held = exchange(rows.reshape(experts, capacity, width), EXPERT).reshape(slots, width)
    twin = swap_cores(held)
    full_x = jnp.where(core == 0, held, twin)
    full_dz = jnp.where(core == 0, twin, held)

    w_gate, w_up, w_down = gate_up[0, 0], gate_up[0, 1], down_proj[0]
    hidden = w_gate.shape[0]
    by_core = jnp.concatenate([w_gate, w_up]).reshape(2 * hidden, far * near, 2, feat)
    own_cols = jnp.where(core == 0, by_core[:, :, 0], by_core[:, :, 1]).reshape(2 * hidden, -1)
    twin_cols = jnp.where(core == 0, by_core[:, :, 1], by_core[:, :, 0]).reshape(2 * hidden, -1)
    own_cols, twin_cols = lax.optimization_barrier((own_cols, twin_cols))

    last = ((1,), (1,))
    gate_part = dot(full_x, w_gate, last)
    up_part = dot(full_x, w_up, last)
    back_grad = dot(full_dz, w_down, last)
    sig_gate = jax.nn.sigmoid(gate_part)
    activated = (gate_part * sig_gate * up_part).astype(BF16)
    grad_gate = (back_grad * up_part * sig_gate * (1.0 + gate_part * (1.0 - sig_gate))).astype(BF16)
    grad_up = (back_grad * gate_part * sig_gate).astype(BF16)

    grads = jnp.concatenate([grad_gate, grad_up], axis=1)
    twin_part = dot(grads, twin_cols, ((1,), (0,))).astype(BF16)
    arrived = swap_cores(twin_part)
    share = (dot(grads, own_cols, ((1,), (0,))) + arrived.astype(F32)).astype(BF16)
    returned = exchange(share.reshape(experts, capacity, -1), EXPERT).reshape(slots, -1)
    summed = dot(returned, picker, ((0,), (0,))).astype(BF16)
    pieces = exchange(summed.reshape(far * near, feat, tok_count), Z)
    grad_tokens = jnp.sum(pieces.astype(F32), axis=0).astype(BF16).T

    first = ((0,), (0,))
    grad_in = jnp.stack([dot(grad_gate, full_x, first), dot(grad_up, full_x, first)]).astype(BF16)
    grad_out = dot(activated, full_dz, first).astype(BF16)
    return grad_tokens, grad_in[None], grad_out[None]


def solution(mesh):
    dp, experts = mesh.devices.shape
    near = 4 if dp % 8 == 0 else 1
    split = Mesh(
        mesh.devices.reshape(dp // (2 * near), near, 2, experts), (FAR, NEAR, CORE, EXPERT)
    )
    shards = (FAR, NEAR, CORE)
    in_specs = (
        P(EXPERT, shards),
        P(EXPERT, shards),
        P(EXPERT, None),
        P(EXPERT, None),
        P(EXPERT, None, shards, None),
        P(EXPERT, shards, None),
    )
    out_specs = (P(EXPERT, shards), P(EXPERT, None, shards, None), P(EXPERT, shards, None))
    return jax.shard_map(
        on_device, mesh=split, in_specs=in_specs, out_specs=out_specs, check_vma=False
    )
```

```python
import jax
import jax.numpy as jnp
from jax import lax
from jax.experimental.layout import Layout, with_layout_constraint
from jax.sharding import PartitionSpec as P

DP, EXPERT = "dp", "expert"
F32, BF16 = jnp.float32, jnp.bfloat16
LAST, FIRST, INNER = ((1,), (1,)), ((0,), (0,)), ((1,), (0,))


def dot(left, right, contract):
    return lax.dot_general(left, right, (contract, ((), ())), preferred_element_type=F32)


def exchange(value, axis, groups=None):
    return lax.all_to_all(
        value, axis, split_axis=0, concat_axis=0, tiled=True, axis_index_groups=groups
    )


def slot_tables(routes, route_weights, experts, capacity):
    tok_count, top_count = routes.shape
    slot_total = experts * capacity
    flat_routes = routes.reshape(-1)
    hot_expert = (flat_routes[:, None] == jnp.arange(experts, dtype=jnp.int32)[None, :]).astype(
        jnp.int32
    )
    earlier = jnp.cumsum(hot_expert, axis=0) - hot_expert
    position = jnp.sum(earlier * hot_expert, axis=1)
    slot_ids = flat_routes * capacity + position
    slot_table = (slot_ids[None, :] == jnp.arange(slot_total, dtype=jnp.int32)[:, None]).astype(F32)
    slot_token = slot_table.reshape(slot_total, tok_count, top_count).sum(axis=2)
    slot_scale = jnp.sum(slot_table * route_weights.reshape(-1)[None, :], axis=1)
    return slot_token.astype(BF16), slot_scale


def on_device(tokens, cotangent, routes, route_weights, gate_up, down_proj):
    dp, experts = lax.axis_size(DP), lax.axis_size(EXPERT)
    depth = dp // 2
    near = 4 if depth % 4 == 0 else 1
    far = depth // near
    core = lax.axis_index(DP) % 2
    tok_count, top_count = routes.shape
    feat = tokens.shape[1]
    width = feat * dp
    capacity = min(tok_count, tok_count * top_count * 4 // (3 * experts))
    slots = experts * capacity

    turn = far // 2
    far_order = [(j + turn) % far for j in range(far)]
    z_order = [f * near + n for f in far_order for n in range(near)]
    far_groups = [[(f * near + n) * 2 + c for f in far_order for c in (0, 1)] for n in range(near)]
    near_groups = [
        [(f * near + n) * 2 + c for n in range(near)] for f in range(far) for c in (0, 1)
    ]
    z_groups = [[z * 2 + c for z in z_order] for c in (0, 1)]

    def swap_cores(value):
        return lax.ppermute(value, DP, [(i, i ^ 1) for i in range(dp)])

    picker, slot_scale = slot_tables(routes, route_weights, experts, capacity)

    block = (2, feat * tok_count // 2)
    both = lax.optimization_barrier(jnp.stack([tokens, cotangent]))
    both = both.transpose(0, 2, 1).reshape(1, 2, *block)
    sent = jnp.broadcast_to(both, (far, 2, *block)).reshape(far * 2, *block)
    column = exchange(sent, DP, far_groups)

    w_gate, w_up, w_down = gate_up[0, 0], gate_up[0, 1], down_proj[0]
    hidden = w_gate.shape[0]
    w_in = jnp.concatenate([w_gate, w_up])
    w_all = jnp.concatenate([w_in, w_down])
    by_core = jnp.roll(w_in.reshape(2 * hidden, depth, 2, feat), -turn * near, axis=1)
    own_cols = jnp.where(core == 0, by_core[:, :, 0], by_core[:, :, 1]).reshape(2 * hidden, -1)
    twin_cols = jnp.where(core == 0, by_core[:, :, 1], by_core[:, :, 0]).reshape(2 * hidden, -1)
    column, w_all, own_cols, twin_cols = lax.optimization_barrier(
        (column, w_all, own_cols, twin_cols)
    )

    column = jnp.broadcast_to(column[None], (near,) + column.shape).reshape(-1, *block)
    column = exchange(column, DP, near_groups)
    column = column.reshape(near, far, 2, feat, tok_count)
    column = jnp.roll(column, turn, axis=1).transpose(1, 0, 2, 3, 4)
    column = with_layout_constraint(column.reshape(width, tok_count), Layout((0, 1)))

    rows = dot(picker, column, LAST).astype(BF16)
    scale = jnp.where(core == 0, 1.0, slot_scale)
    rows = (scale[:, None] * rows.astype(F32)).astype(BF16)
    held = exchange(rows.reshape(experts, capacity, width), EXPERT).reshape(slots, width)
    twin = swap_cores(held)
    from_held, twin = lax.optimization_barrier((dot(held, w_all, LAST), twin))
    from_twin = dot(twin, w_all, LAST)
    full_x = jnp.where(core == 0, held, twin)
    full_dz = jnp.where(core == 0, twin, held)
    from_x = jnp.where(core == 0, from_held, from_twin)
    gate_part, up_part = from_x[:, :hidden], from_x[:, hidden : 2 * hidden]
    back_grad = jnp.where(core == 0, from_twin, from_held)[:, 2 * hidden :]
    sig_gate = jax.nn.sigmoid(gate_part)
    activated = (gate_part * sig_gate * up_part).astype(BF16)
    grad_gate = (back_grad * up_part * sig_gate * (1.0 + gate_part * (1.0 - sig_gate))).astype(BF16)
    grad_up = (back_grad * gate_part * sig_gate).astype(BF16)

    grads = jnp.concatenate([grad_gate, grad_up], axis=1)
    twin_part = dot(grads, twin_cols, INNER).astype(BF16)
    arrived = swap_cores(twin_part)
    share = (dot(grads, own_cols, INNER) + arrived.astype(F32)).astype(BF16)
    returned = exchange(share.reshape(experts, capacity, -1), EXPERT).reshape(slots, -1)
    summed = dot(returned, picker, FIRST).astype(BF16)
    pieces = exchange(summed.reshape(depth, feat, tok_count), DP, z_groups)
    grad_tokens = jnp.sum(pieces.astype(F32), axis=0).astype(BF16).T

    grad_in = jnp.stack([dot(grad_gate, full_x, FIRST), dot(grad_up, full_x, FIRST)]).astype(BF16)
    grad_out = dot(activated, full_dz, FIRST).astype(BF16)
    return grad_tokens, grad_in[None], grad_out[None]


def solution(mesh):
    in_specs = (
        P(EXPERT, DP),
        P(EXPERT, DP),
        P(EXPERT, None),
        P(EXPERT, None),
        P(EXPERT, None, DP, None),
        P(EXPERT, DP, None),
    )
    out_specs = (P(EXPERT, DP), P(EXPERT, None, DP, None), P(EXPERT, DP, None))
    return jax.shard_map(
        on_device, mesh=mesh, in_specs=in_specs, out_specs=out_specs, check_vma=False
    )
```

```python
import jax
import jax.numpy as jnp
from jax import lax
from jax.experimental.layout import Layout, with_layout_constraint
from jax.sharding import PartitionSpec as P

DP, EXPERT = "dp", "expert"
F32, BF16 = jnp.float32, jnp.bfloat16
LAST, FIRST, INNER = ((1,), (1,)), ((0,), (0,)), ((1,), (0,))


def dot(left, right, contract):
    return lax.dot_general(left, right, (contract, ((), ())), preferred_element_type=F32)


hold = lax.optimization_barrier


def exchange(value, axis, groups=None):
    return lax.all_to_all(
        value, axis, split_axis=0, concat_axis=0, tiled=True, axis_index_groups=groups
    )


def slot_tables(routes, route_weights, experts, capacity):
    tok_count, top_count = routes.shape
    slot_total = experts * capacity
    flat_routes = routes.reshape(-1)
    hot_expert = (flat_routes[:, None] == jnp.arange(experts, dtype=jnp.int32)[None, :]).astype(
        jnp.int32
    )
    earlier = jnp.cumsum(hot_expert, axis=0) - hot_expert
    position = jnp.sum(earlier * hot_expert, axis=1)
    slot_ids = flat_routes * capacity + position
    slot_table = (slot_ids[None, :] == jnp.arange(slot_total, dtype=jnp.int32)[:, None]).astype(F32)
    slot_token = slot_table.reshape(slot_total, tok_count, top_count).sum(axis=2)
    slot_scale = jnp.sum(slot_table * route_weights.reshape(-1)[None, :], axis=1)
    return slot_token.astype(BF16), slot_scale


def on_device(tokens, cotangent, routes, route_weights, gate_up, down_proj):
    dp, experts = lax.axis_size(DP), lax.axis_size(EXPERT)
    depth = dp // 2
    near = 4 if depth % 4 == 0 else 1
    far = depth // near
    core = lax.axis_index(DP) % 2
    tok_count, top_count = routes.shape
    feat = tokens.shape[1]
    width = feat * dp
    capacity = min(tok_count, tok_count * top_count * 4 // (3 * experts))
    slots = experts * capacity

    turn = far // 2
    far_order = [(j + turn) % far for j in range(far)]
    z_order = [f * near + n for f in far_order for n in range(near)]
    far_groups = [[(f * near + n) * 2 + c for f in far_order for c in (0, 1)] for n in range(near)]
    near_groups = [
        [(f * near + n) * 2 + c for n in range(near)] for f in range(far) for c in (0, 1)
    ]
    z_groups = [[z * 2 + c for z in z_order] for c in (0, 1)]

    def swap_cores(value):
        return lax.ppermute(value, DP, [(i, i ^ 1) for i in range(dp)])

    block = (2, feat * tok_count // 2)
    both = hold((jnp.stack([tokens, cotangent]),))[0]
    both = both.transpose(0, 2, 1).reshape(1, 2, *block)
    sent = jnp.broadcast_to(both, (far, 2, *block)).reshape(far * 2, *block)
    column = exchange(sent, DP, far_groups)
    picker, slot_scale = slot_tables(routes, route_weights, experts, capacity)
    scale = jnp.where(core == 0, 1.0, slot_scale)
    column, picker, scale, gate_up, down_proj = hold((column, picker, scale, gate_up, down_proj))

    column = jnp.broadcast_to(column[None], (near,) + column.shape).reshape(-1, *block)
    column = exchange(column, DP, near_groups)
    w_gate, w_up, w_down = gate_up[0, 0], gate_up[0, 1], down_proj[0]
    hidden = w_gate.shape[0]
    w_all = jnp.concatenate([w_gate, w_up, w_down])
    column, w_all = hold((column, w_all))

    column = column.reshape(near, far, 2, feat, tok_count)
    column = jnp.roll(column, turn, axis=1).transpose(1, 0, 2, 3, 4)
    column = with_layout_constraint(column.reshape(width, tok_count), Layout((0, 1)))
    rows = dot(picker, column, LAST).astype(BF16)
    rows = (scale[:, None] * rows.astype(F32)).astype(BF16)
    rows, w_all = hold((rows, w_all))
    held = exchange(rows.reshape(experts, capacity, width), EXPERT).reshape(slots, width)
    by_core = w_all[: 2 * hidden].reshape(2 * hidden, depth, 2, feat)
    by_core = jnp.roll(by_core, -turn * near, axis=1)
    own_cols = jnp.where(core == 0, by_core[:, :, 0], by_core[:, :, 1]).reshape(2 * hidden, -1)
    twin_cols = jnp.where(core == 0, by_core[:, :, 1], by_core[:, :, 0]).reshape(2 * hidden, -1)
    held, own_cols, twin_cols = hold((held, own_cols, twin_cols))

    twin = swap_cores(held)
    from_held, twin = hold((dot(held, w_all, LAST), twin))
    from_twin = dot(twin, w_all, LAST)
    full_x = jnp.where(core == 0, held, twin)
    full_dz = jnp.where(core == 0, twin, held)
    from_x = jnp.where(core == 0, from_held, from_twin)
    gate_part, up_part = from_x[:, :hidden], from_x[:, hidden : 2 * hidden]
    back_grad = jnp.where(core == 0, from_twin, from_held)[:, 2 * hidden :]
    sig_gate = jax.nn.sigmoid(gate_part)
    activated = (gate_part * sig_gate * up_part).astype(BF16)
    grad_gate = (back_grad * up_part * sig_gate * (1.0 + gate_part * (1.0 - sig_gate))).astype(BF16)
    grad_up = (back_grad * gate_part * sig_gate).astype(BF16)

    grads = jnp.concatenate([grad_gate, grad_up], axis=1)
    twin_part = dot(grads, twin_cols, INNER).astype(BF16)
    arrived = swap_cores(twin_part)
    share = (dot(grads, own_cols, INNER) + arrived.astype(F32)).astype(BF16)
    returned = exchange(share.reshape(experts, capacity, -1), EXPERT).reshape(slots, -1)
    grad_in = jnp.stack([dot(grad_gate, full_x, FIRST), dot(grad_up, full_x, FIRST)]).astype(BF16)
    grad_out = dot(activated, full_dz, FIRST).astype(BF16)
    returned, grad_in, grad_out = hold((returned, grad_in, grad_out))
    summed = dot(returned, picker, FIRST).astype(BF16)
    pieces = exchange(summed.reshape(depth, feat, tok_count), DP, z_groups)
    grad_tokens = jnp.sum(pieces.astype(F32), axis=0).astype(BF16).T
    return grad_tokens, grad_in[None], grad_out[None]


def solution(mesh):
    in_specs = (
        P(EXPERT, DP),
        P(EXPERT, DP),
        P(EXPERT, None),
        P(EXPERT, None),
        P(EXPERT, None, DP, None),
        P(EXPERT, DP, None),
    )
    out_specs = (P(EXPERT, DP), P(EXPERT, None, DP, None), P(EXPERT, DP, None))
    return jax.shard_map(
        on_device, mesh=mesh, in_specs=in_specs, out_specs=out_specs, check_vma=False
    )
```

```python
import jax
import jax.numpy as jnp
from jax import lax
from jax.experimental.layout import Layout, with_layout_constraint
from jax.sharding import PartitionSpec as P

DP, EXPERT = "dp", "expert"
F32, BF16 = jnp.float32, jnp.bfloat16
LAST, FIRST = ((1,), (1,)), ((0,), (0,))


def dot(left, right, contract, batch=((), ())):
    return lax.dot_general(left, right, (contract, batch), preferred_element_type=F32)


hold = lax.optimization_barrier


def exchange(value, axis, groups=None):
    return lax.all_to_all(
        value, axis, split_axis=0, concat_axis=0, tiled=True, axis_index_groups=groups
    )


def slot_tables(routes, route_weights, experts, capacity):
    tok_count, top_count = routes.shape
    slot_total = experts * capacity
    flat_routes = routes.reshape(-1)
    hot_expert = (flat_routes[:, None] == jnp.arange(experts, dtype=jnp.int32)[None, :]).astype(
        jnp.int32
    )
    earlier = jnp.cumsum(hot_expert, axis=0) - hot_expert
    position = jnp.sum(earlier * hot_expert, axis=1)
    slot_ids = flat_routes * capacity + position
    slot_table = (slot_ids[None, :] == jnp.arange(slot_total, dtype=jnp.int32)[:, None]).astype(F32)
    slot_token = slot_table.reshape(slot_total, tok_count, top_count).sum(axis=2)
    slot_scale = jnp.sum(slot_table * route_weights.reshape(-1)[None, :], axis=1)
    return slot_token.astype(BF16), slot_scale


def on_device(tokens, cotangent, routes, route_weights, gate_up, down_proj):
    dp, experts = lax.axis_size(DP), lax.axis_size(EXPERT)
    depth = dp // 2
    near = 4 if depth % 4 == 0 else 1
    far = depth // near
    pairs = depth // 2
    core = lax.axis_index(DP) & 1
    tok_count, top_count = routes.shape
    feat = tokens.shape[1]
    width = feat * dp
    capacity = min(tok_count, tok_count * top_count * 4 // (3 * experts))
    slots = experts * capacity

    turn = far // 2
    far_order = [(j + turn) % far for j in range(far)]
    far_groups = [[(f * near + n) * 2 + c for f in far_order for c in (0, 1)] for n in range(near)]
    near_groups = [
        [(f * near + n) * 2 + c for n in range(near)] for f in range(far) for c in (0, 1)
    ]
    half_order = [(j + pairs // 2) % pairs for j in range(pairs)]
    half_groups = [[(j * 2 + p) * 2 + c for j in half_order] for p in (0, 1) for c in (0, 1)]
    pair_groups = [
        [((j * 2 + p) * 2 + c) * experts + e for p in (0, 1) for e in range(experts)]
        for j in range(pairs)
        for c in (0, 1)
    ]

    def swap_cores(value):
        return lax.ppermute(value, DP, [(i, i ^ 1) for i in range(dp)])

    block = (2, feat * tok_count // 2)
    both = hold((jnp.stack([tokens, cotangent]),))[0]
    both = both.transpose(0, 2, 1).reshape(1, 2, *block)
    sent = jnp.broadcast_to(both, (far, 2, *block)).reshape(far * 2, *block)
    column = exchange(sent, DP, far_groups)
    picker, slot_scale = slot_tables(routes, route_weights, experts, capacity)
    scale = jnp.where(core == 0, 1.0, slot_scale)
    column, picker, scale, gate_up, down_proj = hold((column, picker, scale, gate_up, down_proj))

    column = jnp.broadcast_to(column[None], (near,) + column.shape).reshape(-1, *block)
    column = exchange(column, DP, near_groups)
    w_gate, w_up, w_down = gate_up[0, 0], gate_up[0, 1], down_proj[0]
    hidden = w_gate.shape[0]
    w_all = jnp.concatenate([w_gate, w_up, w_down])
    by_core = w_all[: 2 * hidden].reshape(2 * hidden, pairs, 2, 2, feat)
    by_core = jnp.roll(by_core, -(pairs // 2), axis=1).transpose(3, 2, 0, 1, 4)
    by_core = by_core.reshape(2, 2, 2 * hidden, pairs * feat)
    own_cols = jnp.where(core == 0, by_core[0], by_core[1])
    twin_cols = jnp.where(core == 0, by_core[1], by_core[0])
    column, w_all, own_cols, twin_cols = hold((column, w_all, own_cols, twin_cols))

    column = column.reshape(near, far, 2, feat, tok_count)
    column = jnp.roll(column, turn, axis=1).transpose(1, 0, 2, 3, 4)
    column = with_layout_constraint(column.reshape(width, tok_count), Layout((0, 1)))
    rows = dot(picker, column, LAST).astype(BF16)
    rows = (scale[:, None] * rows.astype(F32)).astype(BF16)
    held = exchange(rows.reshape(experts, capacity, width), EXPERT).reshape(slots, width)
    twin = swap_cores(held)
    from_held, twin = hold((dot(held, w_all, LAST), twin))
    from_twin = dot(twin, w_all, LAST)
    full_x = jnp.where(core == 0, held, twin)
    full_dz = jnp.where(core == 0, twin, held)
    from_x = jnp.where(core == 0, from_held, from_twin)
    gate_part, up_part = from_x[:, :hidden], from_x[:, hidden : 2 * hidden]
    back_grad = jnp.where(core == 0, from_twin, from_held)[:, 2 * hidden :]
    sig_gate = jax.nn.sigmoid(gate_part)
    activated = (gate_part * sig_gate * up_part).astype(BF16)
    grad_gate = (back_grad * up_part * sig_gate * (1.0 + gate_part * (1.0 - sig_gate))).astype(BF16)
    grad_up = (back_grad * gate_part * sig_gate).astype(BF16)

    grads = jnp.concatenate([grad_gate, grad_up], axis=1)
    grads = jnp.broadcast_to(grads[None], (2,) + grads.shape)
    twin_part = dot(grads, twin_cols, ((2,), (1,)), ((0,), (0,))).astype(BF16)
    arrived = swap_cores(twin_part)
    share = dot(grads, own_cols, ((2,), (1,)), ((0,), (0,))) + arrived.astype(F32)
    share = share.astype(BF16)
    share, grad_gate, grad_up, activated = hold((share, grad_gate, grad_up, activated))
    share = share.reshape(2 * experts, capacity, -1)
    returned = exchange(share, (DP, EXPERT), pair_groups).reshape(2 * slots, -1)
    grad_in = jnp.stack([dot(grad_gate, full_x, FIRST), dot(grad_up, full_x, FIRST)]).astype(BF16)
    grad_out = dot(activated, full_dz, FIRST).astype(BF16)
    returned, grad_in, grad_out = hold((returned, grad_in, grad_out))
    summed = dot(returned, jnp.concatenate([picker, picker]), FIRST).astype(BF16)
    pieces = exchange(summed.reshape(pairs, feat, tok_count), DP, half_groups)
    grad_tokens = jnp.sum(pieces.astype(F32), axis=0).astype(BF16).T
    return grad_tokens, grad_in[None], grad_out[None]


def solution(mesh):
    in_specs = (
        P(EXPERT, DP),
        P(EXPERT, DP),
        P(EXPERT, None),
        P(EXPERT, None),
        P(EXPERT, None, DP, None),
        P(EXPERT, DP, None),
    )
    out_specs = (P(EXPERT, DP), P(EXPERT, None, DP, None), P(EXPERT, DP, None))
    return jax.shard_map(
        on_device, mesh=mesh, in_specs=in_specs, out_specs=out_specs, check_vma=False
    )
```

```python
import jax
import jax.numpy as jnp
from jax import lax
from jax.experimental.layout import Layout, with_layout_constraint
from jax.sharding import PartitionSpec as P

DP, EXPERT = "dp", "expert"
F32, BF16 = jnp.float32, jnp.bfloat16
LAST, FIRST = ((1,), (1,)), ((0,), (0,))


def dot(left, right, contract, batch=((), ())):
    return lax.dot_general(left, right, (contract, batch), preferred_element_type=F32)


hold = lax.optimization_barrier


def exchange(value, axis, groups=None):
    return lax.all_to_all(
        value, axis, split_axis=0, concat_axis=0, tiled=True, axis_index_groups=groups
    )


def slot_tables(routes, route_weights, experts, capacity):
    tok_count, top_count = routes.shape
    slot_total = experts * capacity
    flat_routes = routes.reshape(-1)
    hot_expert = (flat_routes[:, None] == jnp.arange(experts, dtype=jnp.int32)[None, :]).astype(
        jnp.int32
    )
    earlier = jnp.cumsum(hot_expert, axis=0) - hot_expert
    position = jnp.sum(earlier * hot_expert, axis=1)
    slot_ids = flat_routes * capacity + position
    slot_table = (slot_ids[None, :] == jnp.arange(slot_total, dtype=jnp.int32)[:, None]).astype(F32)
    slot_token = slot_table.reshape(slot_total, tok_count, top_count).sum(axis=2)
    slot_scale = jnp.sum(slot_table * route_weights.reshape(-1)[None, :], axis=1)
    return slot_token.astype(BF16), slot_scale


def on_device(tokens, cotangent, routes, route_weights, gate_up, down_proj):
    dp, experts = lax.axis_size(DP), lax.axis_size(EXPERT)
    depth = dp // 2
    near = 4 if depth % 4 == 0 else 1
    far = depth // near
    pairs = depth // 2
    core = lax.axis_index(DP) & 1
    tok_count, top_count = routes.shape
    feat = tokens.shape[1]
    width = feat * dp
    capacity = min(tok_count, tok_count * top_count * 4 // (3 * experts))
    slots = experts * capacity

    turn = far // 2
    far_order = [(j + turn) % far for j in range(far)]
    far_groups = [[(f * near + n) * 2 + c for f in far_order for c in (0, 1)] for n in range(near)]
    near_groups = [
        [(f * near + n) * 2 + c for n in range(near)] for f in range(far) for c in (0, 1)
    ]
    half_order = [(j + pairs // 2) % pairs for j in range(pairs)]
    half_groups = [[(j * 2 + p) * 2 + c for j in half_order] for p in (0, 1) for c in (0, 1)]
    pair_groups = [
        [((j * 2 + p) * 2 + c) * experts + e for p in (0, 1) for e in range(experts)]
        for j in range(pairs)
        for c in (0, 1)
    ]

    def swap_cores(value):
        return lax.ppermute(value, DP, [(i, i ^ 1) for i in range(dp)])

    block = (2, feat * tok_count // 2)
    both = hold((jnp.stack([tokens, cotangent]),))[0]
    both = both.transpose(0, 2, 1).reshape(1, 2, *block)
    sent = jnp.broadcast_to(both, (far, 2, *block)).reshape(far * 2, *block)
    sent, gate_up, down_proj = hold((sent, gate_up, down_proj))
    column = exchange(sent, DP, far_groups)
    w_in = jnp.concatenate([gate_up[0, 0], gate_up[0, 1]])
    w_in, w_down = with_layout_constraint(w_in, Layout((0, 1))), down_proj[0]
    picker, slot_scale = slot_tables(routes, route_weights, experts, capacity)
    scale = jnp.where(core == 0, 1.0, slot_scale)
    column, picker, scale, w_in, w_down = hold((column, picker, scale, w_in, w_down))

    column = jnp.broadcast_to(column[None], (near,) + column.shape).reshape(-1, *block)
    column = exchange(column, DP, near_groups)
    twin_in, twin_down = swap_cores(w_in), swap_cores(w_down)

    column = column.reshape(near, far, 2, feat, tok_count)
    column = jnp.roll(column, turn, axis=1).transpose(1, 0, 2, 3, 4)
    column = with_layout_constraint(column.reshape(width, tok_count), Layout((0, 1)))
    rows = dot(picker, column, LAST).astype(BF16)
    rows = (scale[:, None] * rows.astype(F32)).astype(BF16)
    held = exchange(rows.reshape(experts, capacity, width), EXPERT).reshape(slots, width)

    hidden = w_down.shape[0]
    own = (w_in[:hidden], w_in[hidden:], w_down)
    twin = (twin_in[:hidden], twin_in[hidden:], twin_down)
    unit = 2 * hidden
    w_chip = jnp.where(
        core == 0,
        jnp.concatenate([own[0], twin[0], own[1], twin[1]]),
        jnp.concatenate([twin[2], own[2], twin[2], own[2]]),
    )
    columns = [
        array.reshape(hidden, pairs, 2, 2, feat)[:, :, :, c]
        for array, c in (
            [(own[0], 0), (twin[0], 0), (own[1], 0), (twin[1], 0)]
            + [(twin[0], 1), (own[0], 1), (twin[1], 1), (own[1], 1)]
        )
    ]
    columns = jnp.where(core == 0, jnp.concatenate(columns[:4]), jnp.concatenate(columns[4:]))
    columns = jnp.roll(columns, -(pairs // 2), axis=1).transpose(0, 2, 1, 3)
    columns = columns.reshape(2 * unit, 2 * pairs * feat)
    held, w_chip, columns = hold((held, w_chip, columns))

    mine = dot(w_chip, held, LAST)
    theirs = swap_cores(mine)
    gate_up_part = jnp.where(core == 0, mine, theirs)
    gate_part, up_part = gate_up_part[:unit], gate_up_part[unit:]
    back_grad = jnp.where(core == 0, theirs, mine)[:unit]
    sig_gate = jax.nn.sigmoid(gate_part)
    activated = (gate_part * sig_gate * up_part).astype(BF16)
    grad_gate = (back_grad * up_part * sig_gate * (1.0 + gate_part * (1.0 - sig_gate))).astype(BF16)
    grad_up = (back_grad * gate_part * sig_gate).astype(BF16)

    share = dot(jnp.concatenate([grad_gate, grad_up]), columns, FIRST).astype(BF16)
    share = share.reshape(slots, 2, -1).transpose(1, 0, 2)
    share, grad_gate, grad_up, activated, held = hold((share, grad_gate, grad_up, activated, held))
    share = share.reshape(2 * experts, capacity, -1)
    returned = exchange(share, (DP, EXPERT), pair_groups).reshape(2 * slots, -1)
    other = swap_cores(held)
    full_x = jnp.where(core == 0, held, other)
    full_dz = jnp.where(core == 0, other, held)
    grad_gate, grad_up, activated = (
        jnp.where(core == 0, both[:hidden], both[hidden:])
        for both in (grad_gate, grad_up, activated)
    )
    plain = ((1,), (0,))
    grad_in = jnp.stack([dot(grad_gate, full_x, plain), dot(grad_up, full_x, plain)]).astype(BF16)
    grad_out = dot(activated, full_dz, plain).astype(BF16)
    returned, grad_in, grad_out = hold((returned, grad_in, grad_out))
    summed = dot(returned, jnp.concatenate([picker, picker]), FIRST).astype(BF16)
    pieces = exchange(summed.reshape(pairs, feat, tok_count), DP, half_groups)
    grad_tokens = jnp.sum(pieces.astype(F32), axis=0).astype(BF16).T
    return grad_tokens, grad_in[None], grad_out[None]


def solution(mesh):
    in_specs = (
        P(EXPERT, DP),
        P(EXPERT, DP),
        P(EXPERT, None),
        P(EXPERT, None),
        P(EXPERT, None, DP, None),
        P(EXPERT, DP, None),
    )
    out_specs = (P(EXPERT, DP), P(EXPERT, None, DP, None), P(EXPERT, DP, None))
    return jax.shard_map(
        on_device, mesh=mesh, in_specs=in_specs, out_specs=out_specs, check_vma=False
    )
```

```python
import jax
import jax.numpy as jnp
from jax import lax
from jax.experimental.layout import Layout, with_layout_constraint
from jax.sharding import PartitionSpec as P

DP, EXPERT = "dp", "expert"
F32, BF16 = jnp.float32, jnp.bfloat16
LAST, FIRST, PLAIN = ((1,), (1,)), ((0,), (0,)), ((1,), (0,))


def dot(left, right, contract, batch=((), ())):
    return lax.dot_general(left, right, (contract, batch), preferred_element_type=F32)


hold = lax.optimization_barrier


def exchange(value, axis, groups=None):
    return lax.all_to_all(
        value, axis, split_axis=0, concat_axis=0, tiled=True, axis_index_groups=groups
    )


def slot_tables(routes, route_weights, experts, capacity):
    tok_count, top_count = routes.shape
    slot_total = experts * capacity
    flat_routes = routes.reshape(-1)
    hot_expert = (flat_routes[:, None] == jnp.arange(experts, dtype=jnp.int32)[None, :]).astype(
        jnp.int32
    )
    earlier = jnp.cumsum(hot_expert, axis=0) - hot_expert
    position = jnp.sum(earlier * hot_expert, axis=1)
    slot_ids = flat_routes * capacity + position
    slot_table = (slot_ids[None, :] == jnp.arange(slot_total, dtype=jnp.int32)[:, None]).astype(F32)
    slot_token = slot_table.reshape(slot_total, tok_count, top_count).sum(axis=2)
    slot_scale = jnp.sum(slot_table * route_weights.reshape(-1)[None, :], axis=1)
    return slot_token.astype(BF16), slot_scale


def on_device(tokens, cotangent, routes, route_weights, gate_up, down_proj):
    dp, experts = lax.axis_size(DP), lax.axis_size(EXPERT)
    depth = dp // 2
    near = 4 if depth % 4 == 0 else 1
    far = depth // near
    pairs = depth // 2
    core = lax.axis_index(DP) & 1
    tok_count, top_count = routes.shape
    feat = tokens.shape[1]
    width = feat * dp
    capacity = min(tok_count, tok_count * top_count * 4 // (3 * experts))
    slots = experts * capacity

    turn = far // 2
    far_order = [(j + turn) % far for j in range(far)]
    far_groups = [[(f * near + n) * 2 + c for f in far_order for c in (0, 1)] for n in range(near)]
    near_groups = [
        [(f * near + n) * 2 + c for n in range(near)] for f in range(far) for c in (0, 1)
    ]
    half_order = [(j + pairs // 2) % pairs for j in range(pairs)]
    half_groups = [[(j * 2 + p) * 2 + c for j in half_order] for p in (0, 1) for c in (0, 1)]
    pair_groups = [
        [((j * 2 + p) * 2 + c) * experts + e for p in (0, 1) for e in range(experts)]
        for j in range(pairs)
        for c in (0, 1)
    ]

    def swap_cores(value):
        return lax.ppermute(value, DP, [(i, i ^ 1) for i in range(dp)])

    block = (2, feat * tok_count // 2)
    both = hold((jnp.stack([tokens, cotangent]),))[0]
    both = both.transpose(0, 2, 1).reshape(1, 2, *block)
    sent = jnp.broadcast_to(both, (far, 2, *block)).reshape(far * 2, *block)
    sent, gate_up, down_proj = hold((sent, gate_up, down_proj))
    column = exchange(sent, DP, far_groups)
    w_in = jnp.concatenate([gate_up[0, 0], gate_up[0, 1]])
    w_in, w_down = with_layout_constraint(w_in, Layout((0, 1))), down_proj[0]
    picker, slot_scale = slot_tables(routes, route_weights, experts, capacity)
    scale = jnp.where(core == 0, 1.0, slot_scale)
    column, picker, scale, w_in, w_down = hold((column, picker, scale, w_in, w_down))

    column = jnp.broadcast_to(column[None], (near,) + column.shape).reshape(-1, *block)
    column = exchange(column, DP, near_groups)
    twin_in, twin_down = swap_cores(w_in), swap_cores(w_down)

    column = column.reshape(near, far, 2, feat, tok_count)
    column = jnp.roll(column, turn, axis=1).transpose(1, 0, 2, 3, 4)
    column = with_layout_constraint(column.reshape(width, tok_count), Layout((0, 1)))
    rows = dot(picker, column, LAST).astype(BF16)
    rows = (scale[:, None] * rows.astype(F32)).astype(BF16)
    rows, twin_in, twin_down = hold((rows, twin_in, twin_down))
    held = exchange(rows.reshape(experts, capacity, width), EXPERT).reshape(slots, width)

    hidden = w_down.shape[0]
    unit = 2 * hidden
    w_pair = with_layout_constraint(jnp.concatenate([w_in, twin_in]), Layout((0, 1)))
    gap = jnp.zeros((hidden, width), BF16)
    w_other = jnp.concatenate([w_down, gap, twin_down, gap])
    is_gate = (jnp.arange(2 * unit) % unit < hidden)[:, None]
    w_chip = jnp.where((core == 1) & is_gate, w_other, w_pair)
    w_chip = with_layout_constraint(w_chip, Layout((0, 1)))
    w_chip = with_layout_constraint(hold((w_chip,))[0], Layout((1, 0)))
    part = (pairs // 2) * feat
    place = jnp.arange(2 * part)
    origin = ((place % part // feat * 2 + place // part) * 2 + core) * feat + place % feat
    pick = (jnp.arange(4 * part)[:, None] == origin[None, :]).astype(BF16)
    halves = [dot(w_pair[:, i : i + 4 * part], pick, PLAIN).astype(BF16) for i in (4 * part, 0)]
    columns = jnp.concatenate(
        [half[:, p * part : (p + 1) * part] for p in (0, 1) for half in halves], axis=1
    )
    held, w_chip, columns = hold((held, w_chip, columns))

    mine = hold((dot(held, w_chip, LAST),))[0].T
    theirs = swap_cores(mine)
    grad_gate, grad_up, activated = [], [], []
    for mine_here, theirs_here in ((mine[:unit], theirs[unit:]), (mine[unit:], theirs[:unit])):
        gate_up_part = jnp.where(core == 0, mine_here, theirs_here)
        gate_part, up_part = gate_up_part[:hidden], gate_up_part[hidden:]
        back_grad = jnp.where(core == 0, theirs_here, mine_here)[:hidden]
        sig_gate = jax.nn.sigmoid(gate_part)
        activated.append((gate_part * sig_gate * up_part).astype(BF16))
        slope = sig_gate * (1.0 + gate_part * (1.0 - sig_gate))
        grad_gate.append((back_grad * up_part * slope).astype(BF16))
        grad_up.append((back_grad * gate_part * sig_gate).astype(BF16))

    grads = jnp.concatenate([grad_gate[0], grad_up[0], grad_gate[1], grad_up[1]])
    share = dot(grads, columns, FIRST).astype(BF16)
    share = share.reshape(slots, 2, -1).transpose(1, 0, 2)
    share, grad_gate, grad_up, activated, held = hold(
        (share, grad_gate[0], grad_up[0], activated[0], held)
    )
    share = share.reshape(2 * experts, capacity, -1)
    returned = exchange(share, (DP, EXPERT), pair_groups).reshape(2 * slots, -1)
    other = swap_cores(held)
    full_x = jnp.where(core == 0, held, other)
    full_dz = jnp.where(core == 0, other, held)
    grad_in = jnp.stack([dot(grad_gate, full_x, PLAIN), dot(grad_up, full_x, PLAIN)]).astype(BF16)
    grad_out = dot(activated, full_dz, PLAIN).astype(BF16)
    returned, grad_in, grad_out = hold((returned, grad_in, grad_out))
    summed = dot(returned, jnp.concatenate([picker, picker]), FIRST).astype(BF16)
    pieces = exchange(summed.reshape(pairs, feat, tok_count), DP, half_groups)
    grad_tokens = jnp.sum(pieces.astype(F32), axis=0).astype(BF16).T
    return grad_tokens, grad_in[None], grad_out[None]


def solution(mesh):
    in_specs = (
        P(EXPERT, DP),
        P(EXPERT, DP),
        P(EXPERT, None),
        P(EXPERT, None),
        P(EXPERT, None, DP, None),
        P(EXPERT, DP, None),
    )
    out_specs = (P(EXPERT, DP), P(EXPERT, None, DP, None), P(EXPERT, DP, None))
    return jax.shard_map(
        on_device, mesh=mesh, in_specs=in_specs, out_specs=out_specs, check_vma=False
    )
```

```python
import jax
import jax.numpy as jnp
from jax import lax
from jax.experimental.layout import Layout, with_layout_constraint
from jax.sharding import PartitionSpec as P

DP, EXPERT = "dp", "expert"
F32, BF16 = jnp.float32, jnp.bfloat16
LAST, FIRST, PLAIN = ((1,), (1,)), ((0,), (0,)), ((1,), (0,))


def dot(left, right, contract, batch=((), ())):
    return lax.dot_general(left, right, (contract, batch), preferred_element_type=F32)


hold = lax.optimization_barrier


def exchange(value, axis, groups=None):
    return lax.all_to_all(
        value, axis, split_axis=0, concat_axis=0, tiled=True, axis_index_groups=groups
    )


def slot_tables(routes, route_weights, experts, capacity):
    tok_count, top_count = routes.shape
    slot_total = experts * capacity
    flat_routes = routes.reshape(-1)
    hot_expert = (flat_routes[:, None] == jnp.arange(experts, dtype=jnp.int32)[None, :]).astype(
        jnp.int32
    )
    earlier = jnp.cumsum(hot_expert, axis=0) - hot_expert
    position = jnp.sum(earlier * hot_expert, axis=1)
    slot_ids = flat_routes * capacity + position
    slot_table = (slot_ids[None, :] == jnp.arange(slot_total, dtype=jnp.int32)[:, None]).astype(F32)
    slot_token = slot_table.reshape(slot_total, tok_count, top_count).sum(axis=2)
    slot_scale = jnp.sum(slot_table * route_weights.reshape(-1)[None, :], axis=1)
    return slot_token.astype(BF16), slot_scale


def on_device(tokens, cotangent, routes, route_weights, gate_up, down_proj):
    dp, experts = lax.axis_size(DP), lax.axis_size(EXPERT)
    depth = dp // 2
    near = 4 if depth % 4 == 0 else 1
    far = depth // near
    pairs = depth // 2
    core = lax.axis_index(DP) & 1
    tok_count, top_count = routes.shape
    feat = tokens.shape[1]
    width = feat * dp
    capacity = min(tok_count, tok_count * top_count * 4 // (3 * experts))
    slots = experts * capacity

    turn, tilt = far // 2, near // 2
    far_order = [(j + turn) % far for j in range(far)]
    far_groups = [[(f * near + n) * 2 + c for f in far_order for c in (0, 1)] for n in range(near)]
    near_groups = [
        [(f * near + (n + tilt) % near) * 2 + c for n in range(near)]
        for f in range(far)
        for c in (0, 1)
    ]
    half_order = [(j + pairs // 2) % pairs for j in range(pairs)]
    half_groups = [[(j * 2 + p) * 2 + c for j in half_order] for p in (0, 1) for c in (0, 1)]
    pair_groups = [
        [((j * 2 + p) * 2 + c) * experts + e for p in (0, 1) for e in range(experts)]
        for j in range(pairs)
        for c in (0, 1)
    ]

    def swap_cores(value):
        return lax.ppermute(value, DP, [(i, i ^ 1) for i in range(dp)])

    block = (2, feat * tok_count // 2)
    both = hold((jnp.stack([tokens, cotangent]),))[0]
    both = both.transpose(0, 2, 1).reshape(1, 2, *block)
    sent = jnp.broadcast_to(both, (far, 2, *block)).reshape(far * 2, *block)
    sent, gate_up, down_proj = hold((sent, gate_up, down_proj))
    column = exchange(sent, DP, far_groups)
    w_in = jnp.concatenate([gate_up[0, 0], gate_up[0, 1]])
    w_in, w_down = with_layout_constraint(w_in, Layout((0, 1))), down_proj[0]
    picker, slot_scale = slot_tables(routes, route_weights, experts, capacity)
    scale = jnp.where(core == 0, 1.0, slot_scale)
    column, picker, scale, w_in, w_down = hold((column, picker, scale, w_in, w_down))

    column = jnp.broadcast_to(column[None], (near,) + column.shape).reshape(-1, *block)
    column = exchange(column, DP, near_groups)
    column = jnp.roll(column, tilt * far * 2, axis=0)
    twin_in, twin_down = swap_cores(w_in), swap_cores(w_down)

    column = column.reshape(near, far, 2, feat, tok_count)
    column = jnp.roll(column, turn, axis=1).transpose(1, 0, 2, 3, 4)
    column = with_layout_constraint(column.reshape(width, tok_count), Layout((0, 1)))
    rows = dot(picker, column, LAST).astype(BF16)
    rows = (scale[:, None] * rows.astype(F32)).astype(BF16)
    rows, twin_in, twin_down = hold((rows, twin_in, twin_down))
    held = exchange(rows.reshape(experts, capacity, width), EXPERT).reshape(slots, width)

    hidden = w_down.shape[0]
    unit = 2 * hidden
    w_pair = with_layout_constraint(jnp.concatenate([w_in, twin_in]), Layout((0, 1)))
    gap = jnp.zeros((hidden, width), BF16)
    w_other = jnp.concatenate([w_down, gap, twin_down, gap])
    is_gate = (jnp.arange(2 * unit) % unit < hidden)[:, None]
    w_chip = jnp.where((core == 1) & is_gate, w_other, w_pair)
    w_chip = with_layout_constraint(w_chip, Layout((0, 1)))
    w_chip = with_layout_constraint(hold((w_chip,))[0], Layout((1, 0)))
    part = (pairs // 2) * feat
    place = jnp.arange(2 * part)
    origin = ((place % part // feat * 2 + place // part) * 2 + core) * feat + place % feat
    pick = (jnp.arange(4 * part)[:, None] == origin[None, :]).astype(BF16)
    halves = [dot(w_pair[:, i : i + 4 * part], pick, PLAIN).astype(BF16) for i in (4 * part, 0)]
    columns = jnp.concatenate(
        [half[:, p * part : (p + 1) * part] for p in (0, 1) for half in halves], axis=1
    )
    held, w_chip, columns = hold((held, w_chip, columns))

    mine = with_layout_constraint(dot(held, w_chip, LAST), Layout((0, 1)))
    mine = with_layout_constraint(hold((mine,))[0].T, Layout((0, 1)))
    theirs = swap_cores(mine)
    grad_gate, grad_up, activated = [], [], []
    for mine_here, theirs_here in ((mine[:unit], theirs[unit:]), (mine[unit:], theirs[:unit])):
        gate_up_part = jnp.where(core == 0, mine_here, theirs_here)
        gate_part, up_part = gate_up_part[:hidden], gate_up_part[hidden:]
        back_grad = jnp.where(core == 0, theirs_here, mine_here)[:hidden]
        sig_gate = jax.nn.sigmoid(gate_part)
        activated.append((gate_part * sig_gate * up_part).astype(BF16))
        slope = sig_gate * (1.0 + gate_part * (1.0 - sig_gate))
        grad_gate.append((back_grad * up_part * slope).astype(BF16))
        grad_up.append((back_grad * gate_part * sig_gate).astype(BF16))

    grads = jnp.concatenate([grad_gate[0], grad_up[0], grad_gate[1], grad_up[1]])
    share = dot(grads, columns, FIRST).astype(BF16)
    share = share.reshape(slots, 2, -1).transpose(1, 0, 2)
    share, grad_gate, grad_up, activated, held = hold(
        (share, grad_gate[0], grad_up[0], activated[0], held)
    )
    share = share.reshape(2 * experts, capacity, -1)
    returned = exchange(share, (DP, EXPERT), pair_groups).reshape(2 * slots, -1)
    other = swap_cores(held)
    full_x = jnp.where(core == 0, held, other)
    full_dz = jnp.where(core == 0, other, held)
    grad_in = jnp.stack([dot(grad_gate, full_x, PLAIN), dot(grad_up, full_x, PLAIN)]).astype(BF16)
    grad_out = dot(activated, full_dz, PLAIN).astype(BF16)
    returned, grad_in, grad_out = hold((returned, grad_in, grad_out))
    summed = dot(returned, jnp.concatenate([picker, picker]), FIRST).astype(BF16)
    pieces = exchange(summed.reshape(pairs, feat, tok_count), DP, half_groups)
    grad_tokens = jnp.sum(pieces.astype(F32), axis=0).astype(BF16).T
    return grad_tokens, grad_in[None], grad_out[None]


def solution(mesh):
    in_specs = (
        P(EXPERT, DP),
        P(EXPERT, DP),
        P(EXPERT, None),
        P(EXPERT, None),
        P(EXPERT, None, DP, None),
        P(EXPERT, DP, None),
    )
    out_specs = (P(EXPERT, DP), P(EXPERT, None, DP, None), P(EXPERT, DP, None))
    return jax.shard_map(
        on_device, mesh=mesh, in_specs=in_specs, out_specs=out_specs, check_vma=False
    )
```

```python
import jax
import jax.numpy as jnp
from jax import lax
from jax.experimental.layout import Layout, with_layout_constraint
from jax.sharding import PartitionSpec as P

DP, EXPERT = "dp", "expert"
F32, BF16 = jnp.float32, jnp.bfloat16
LAST, FIRST, PLAIN = ((1,), (1,)), ((0,), (0,)), ((1,), (0,))


def dot(left, right, contract, batch=((), ())):
    return lax.dot_general(left, right, (contract, batch), preferred_element_type=F32)


hold = lax.optimization_barrier


def exchange(value, axis, groups=None):
    return lax.all_to_all(
        value, axis, split_axis=0, concat_axis=0, tiled=True, axis_index_groups=groups
    )


def slot_tables(routes, route_weights, experts, capacity):
    tok_count, top_count = routes.shape
    slot_total = experts * capacity
    flat_routes = routes.reshape(-1)
    hot_expert = (flat_routes[:, None] == jnp.arange(experts, dtype=jnp.int32)[None, :]).astype(
        jnp.int32
    )
    earlier = jnp.cumsum(hot_expert, axis=0) - hot_expert
    position = jnp.sum(earlier * hot_expert, axis=1)
    slot_ids = flat_routes * capacity + position
    slot_table = (slot_ids[None, :] == jnp.arange(slot_total, dtype=jnp.int32)[:, None]).astype(F32)
    slot_token = slot_table.reshape(slot_total, tok_count, top_count).sum(axis=2)
    slot_scale = jnp.sum(slot_table * route_weights.reshape(-1)[None, :], axis=1)
    return slot_token.astype(BF16), slot_scale


def on_device(tokens, cotangent, routes, route_weights, gate_up, down_proj):
    dp, experts = lax.axis_size(DP), lax.axis_size(EXPERT)
    depth = dp // 2
    near = 4 if depth % 4 == 0 else 1
    far = depth // near
    pairs = depth // 2
    core = lax.axis_index(DP) & 1
    tok_count, top_count = routes.shape
    feat = tokens.shape[1]
    width = feat * dp
    capacity = min(tok_count, tok_count * top_count * 4 // (3 * experts))
    slots = experts * capacity

    turn, tilt = far // 2, near // 2
    far_order = [(j + turn) % far for j in range(far)]
    far_groups = [[(f * near + n) * 2 + c for f in far_order for c in (0, 1)] for n in range(near)]
    near_groups = [
        [(f * near + (n + tilt) % near) * 2 + c for n in range(near)]
        for f in range(far)
        for c in (0, 1)
    ]
    half_order = [(j + pairs // 2) % pairs for j in range(pairs)]
    half_groups = [[(j * 2 + p) * 2 + c for j in half_order] for p in (0, 1) for c in (0, 1)]
    pair_groups = [
        [((j * 2 + p) * 2 + c) * experts + e for p in (0, 1) for e in range(experts)]
        for j in range(pairs)
        for c in (0, 1)
    ]

    def swap_cores(value):
        return lax.ppermute(value, DP, [(i, i ^ 1) for i in range(dp)])

    block = (2, feat * tok_count // 2)
    both = hold((jnp.stack([tokens, cotangent]),))[0]
    both = both.transpose(0, 2, 1).reshape(1, 2, *block)
    sent = jnp.broadcast_to(both, (far, 2, *block)).reshape(far * 2, *block)
    sent, gate_up, down_proj = hold((sent, gate_up, down_proj))
    column = exchange(sent, DP, far_groups)
    w_in = jnp.concatenate([gate_up[0, 0], gate_up[0, 1]])
    w_in, w_down = with_layout_constraint(w_in, Layout((0, 1))), down_proj[0]
    picker, slot_scale = slot_tables(routes, route_weights, experts, capacity)
    scale = jnp.where(core == 0, 1.0, slot_scale)
    column, picker, scale, w_in, w_down = hold((column, picker, scale, w_in, w_down))

    column = jnp.broadcast_to(column[None], (near,) + column.shape).reshape(-1, *block)
    column = exchange(column, DP, near_groups)
    column = jnp.roll(column, tilt * far * 2, axis=0)
    twin_in, twin_down = swap_cores(w_in), swap_cores(w_down)

    column = column.reshape(near, far, 2, feat, tok_count)
    column = jnp.roll(column, turn, axis=1).transpose(1, 0, 2, 3, 4)
    column = with_layout_constraint(column.reshape(width, tok_count), Layout((0, 1)))
    rows = dot(picker, column, LAST).astype(BF16)
    rows = (scale[:, None] * rows.astype(F32)).astype(BF16)
    rows, twin_in, twin_down = hold((rows, twin_in, twin_down))
    held = exchange(rows.reshape(experts, capacity, width), EXPERT).reshape(slots, width)

    hidden = w_down.shape[0]
    unit = 2 * hidden
    w_pair = with_layout_constraint(jnp.concatenate([w_in, twin_in]), Layout((0, 1)))
    gap = jnp.zeros((hidden, width), BF16)
    takes_down = (core == 1) & (jnp.arange(unit) < hidden)[:, None]
    w_own = jnp.where(takes_down, jnp.concatenate([w_down, gap]), w_in)
    w_twin = jnp.where(takes_down, jnp.concatenate([twin_down, gap]), twin_in)
    part = (pairs // 2) * feat
    place = jnp.arange(2 * part)
    origin = ((place % part // feat * 2 + place // part) * 2 + core) * feat + place % feat
    pick = (jnp.arange(4 * part)[:, None] == origin[None, :]).astype(BF16)
    halves = [dot(w_pair[:, i : i + 4 * part], pick, PLAIN).astype(BF16) for i in (4 * part, 0)]
    columns = jnp.concatenate(
        [half[:, p * part : (p + 1) * part] for p in (0, 1) for half in halves], axis=1
    )
    held, w_own, w_twin, columns = hold((held, w_own, w_twin, columns))

    mine = jnp.concatenate([dot(w_own, held, LAST), dot(w_twin, held, LAST)])
    theirs = swap_cores(mine)
    grad_gate, grad_up, activated = [], [], []
    for mine_here, theirs_here in ((mine[:unit], theirs[unit:]), (mine[unit:], theirs[:unit])):
        gate_up_part = jnp.where(core == 0, mine_here, theirs_here)
        gate_part, up_part = gate_up_part[:hidden], gate_up_part[hidden:]
        back_grad = jnp.where(core == 0, theirs_here, mine_here)[:hidden]
        sig_gate = jax.nn.sigmoid(gate_part)
        activated.append((gate_part * sig_gate * up_part).astype(BF16))
        slope = sig_gate * (1.0 + gate_part * (1.0 - sig_gate))
        grad_gate.append((back_grad * up_part * slope).astype(BF16))
        grad_up.append((back_grad * gate_part * sig_gate).astype(BF16))

    grads = jnp.concatenate([grad_gate[0], grad_up[0], grad_gate[1], grad_up[1]])
    share = dot(grads, columns, FIRST).astype(BF16)
    share = share.reshape(slots, 2, -1).transpose(1, 0, 2)
    share, grad_gate, grad_up, activated, held = hold(
        (share, grad_gate[0], grad_up[0], activated[0], held)
    )
    share = share.reshape(2 * experts, capacity, -1)
    returned = exchange(share, (DP, EXPERT), pair_groups).reshape(2 * slots, -1)
    other = swap_cores(held)
    full_x = jnp.where(core == 0, held, other)
    full_dz = jnp.where(core == 0, other, held)
    grad_in = jnp.stack([dot(grad_gate, full_x, PLAIN), dot(grad_up, full_x, PLAIN)]).astype(BF16)
    grad_out = dot(activated, full_dz, PLAIN).astype(BF16)
    returned, grad_in, grad_out = hold((returned, grad_in, grad_out))
    summed = dot(returned, jnp.concatenate([picker, picker]), FIRST).astype(BF16)
    pieces = exchange(summed.reshape(pairs, feat, tok_count), DP, half_groups)
    grad_tokens = jnp.sum(pieces.astype(F32), axis=0).astype(BF16).T
    return grad_tokens, grad_in[None], grad_out[None]


def solution(mesh):
    in_specs = (
        P(EXPERT, DP),
        P(EXPERT, DP),
        P(EXPERT, None),
        P(EXPERT, None),
        P(EXPERT, None, DP, None),
        P(EXPERT, DP, None),
    )
    out_specs = (P(EXPERT, DP), P(EXPERT, None, DP, None), P(EXPERT, DP, None))
    return jax.shard_map(
        on_device, mesh=mesh, in_specs=in_specs, out_specs=out_specs, check_vma=False
    )
```
